32 devices in a mesh: leaf: 16 (over z, y, x), cone: 2 (over core).
Axes of the slice: x: 2, y: 2, z: 4, core: 2. Of those that a mesh axis runs over, the one named last changes fastest.
Arguments:
- coefficients: bfloat16 [128, 4, 3, 32, 256], P('leaf', 'cone'), may hold values from -6 to 6
- local_to_target: bfloat16 [128, 4, 256, 768], P('leaf', 'cone'), may hold values from -0.1875 to 0.1875
- send_map: int32 [16, 16, 32], P('leaf'), may hold values from -1 to 255, as said below
- test_weight: bfloat16 [16, 16, 32, 108], P('leaf'), may hold values from -1 to 1
- slot_edge: int32 [3, 16, 16, 32], P(None, 'leaf'), may hold values from -1 to 383, as said below
- shared_edges: int32 [16, 2, 32], P('leaf'), may hold values from 0 to 383, as said below
Outputs:
- tested: float32 [2, 32, 6144], P(None, 'cone', 'leaf')
The draws below stay inside these ranges and needn't reach their ends.
Inputs may be any that keep to these rules, and one draw needn't show every extreme that they name: Each of the 256 triangles of a leaf device s stands in exactly one slot of send_map[s]; every other slot is -1. In every draw, each leaf device fills all 32 slots of its block to some owner. slot_edge[e, d, s, n] is -1 exactly where send_map[s, d, n] is -1. The 64 numbers of shared_edges[d] are distinct.
All inputs are finite; a program needn't handle non-finite values.
Results may differ from the reference program's by a relative error of at most 0.0029.
Values may be sent and summed in bfloat16 or wider, within the bound.
A program may use at most 64 MiB of HBM per device.

```python
import jax
import jax.numpy as jnp
from jax import lax

R = 128
QUAD = 12
NRHS = 32
CONES = 4
LEAVES = 128
PTS = 768
TRI_DEV = 256
EDGE_DEV = 384
SHARE = 32
CAP = 32
N_LEAF = 16


def route_plan(key):
    slot_count = N_LEAF * CAP
    base_key = jax.random.fold_in(key, 7)
    slot_owner = jnp.arange(slot_count) // CAP

    def for_source(source):
        source_key = jax.random.fold_in(base_key, 1000 + source)
        slot_order = jax.random.permutation(jax.random.fold_in(source_key, 1), slot_count)
        full_owner = (source + N_LEAF // 2) % N_LEAF
        slot_score = jnp.where(slot_owner == full_owner, slot_order - slot_count * slot_count, slot_order)
        slot_rank = jnp.argsort(jnp.argsort(slot_score, stable=True), stable=True)
        triangle_order = jax.random.permutation(jax.random.fold_in(source_key, 3), TRI_DEV)
        chosen = triangle_order[jnp.minimum(slot_rank, TRI_DEV - 1)]
        slot_value = jnp.where(slot_rank < TRI_DEV, chosen, -1)
        return slot_value.astype(jnp.int32).reshape(N_LEAF, CAP)
    return jax.vmap(for_source)(jnp.arange(N_LEAF))


def draw_send_map(key, part):
    return route_plan(key)


def draw_slot_edge(key, part):
    plan = route_plan(key)
    is_live = jnp.transpose(plan, (1, 0, 2)) >= 0
    edge_draw = jax.random.randint(jax.random.fold_in(key, 11), (3, N_LEAF, N_LEAF, CAP), 0, EDGE_DEV)
    return jnp.where(is_live[None], edge_draw, -1).astype(jnp.int32)


def draw_shared_edges(key, part):
    base_key = jax.random.fold_in(key, 23)

    def for_owner(owner):
        order = jax.random.permutation(jax.random.fold_in(base_key, owner), EDGE_DEV)
        return order[:2 * SHARE].reshape(2, SHARE)
    return jax.vmap(for_owner)(jnp.arange(N_LEAF)).astype(jnp.int32)


def steps_of(own_key, shape, cuts, least, high):
    gain = 1.0
    for dim, parts in cuts:
        draws = jax.random.uniform(jax.random.fold_in(jax.random.fold_in(own_key, 6), dim), (parts,), jnp.float32, least / len(cuts), high / len(cuts))
        gain = gain * jnp.repeat(jnp.exp(draws), shape[dim] // parts).reshape((-1,) + (1,) * (len(shape) - 1 - dim))
    return gain


def gaussian(own_key, shape, scale, limit, cuts=(), kind=jnp.bfloat16):
    factor_of = steps_of(own_key, shape, cuts, -0.22, 0.18) if cuts else 1.0
    result = jax.random.normal(own_key, shape, jnp.float32) * scale * factor_of
    return jnp.minimum(jnp.maximum(result, -limit), limit).astype(kind)


def setup_inputs(seed: int = 0) -> dict:
    key_of = jax.random.split(jax.random.key(seed), 7)
    coefficients = gaussian(key_of[0], (LEAVES, CONES, 3, NRHS, 2 * R), 1.0, 6.0, ((0, 16), (1, 2)))
    local_to_target = gaussian(key_of[1], (LEAVES, CONES, 2 * R, PTS), (2 * R * CONES) ** -0.5, 0.1875, ((0, 16), (1, 2)))
    send_map = draw_send_map(jax.random.fold_in(key_of[6], 71), 0)
    test_weight = gaussian(key_of[3], (N_LEAF, N_LEAF, CAP, 9 * QUAD), (3 * QUAD) ** -0.5, 1.0, ((0, 16),))
    slot_edge = draw_slot_edge(jax.random.fold_in(key_of[6], 71), 0)
    shared_edges = draw_shared_edges(jax.random.fold_in(key_of[6], 71), 0)
    return dict(coefficients=coefficients, local_to_target=local_to_target, send_map=send_map, test_weight=test_weight, slot_edge=slot_edge, shared_edges=shared_edges)


def leaf_field(leaf_pair):
    coeff_leaf, operator_leaf = leaf_pair
    summed = jnp.einsum('kchr,krq->qch', coeff_leaf.astype(jnp.float32), operator_leaf.astype(jnp.float32))
    return summed.astype(jnp.bfloat16)


def reference(coefficients, local_to_target, send_map, test_weight, slot_edge, shared_edges):
    field = lax.map(leaf_field, (coefficients, local_to_target))
    tri_field = field.reshape(N_LEAF, TRI_DEV, 2 * QUAD * 3 * NRHS)
    source_rows = jnp.arange(N_LEAF)[:, None]

    def owner_sums(owner):
        owner_rows = lax.dynamic_index_in_dim(send_map, owner, 1, keepdims=False)
        is_live = owner_rows >= 0
        safe_rows = jnp.where(is_live, owner_rows, 0)
        picked = tri_field[source_rows, safe_rows]
        picked = jnp.where(is_live[:, :, None], picked, jnp.zeros((), jnp.bfloat16))
        slot_values = picked.reshape(N_LEAF, CAP, QUAD, 2, 3, NRHS).astype(jnp.float32)
        weights = lax.dynamic_index_in_dim(test_weight, owner, 0, keepdims=False)
        weights = weights.reshape(N_LEAF, CAP, 3, QUAD, 3).astype(jnp.float32)
        partial_value = jnp.einsum('scepk,scpikh->sceih', weights, slot_values)
        edge_ids = jnp.transpose(lax.dynamic_index_in_dim(slot_edge, owner, 1, keepdims=False), (1, 2, 0))
        edge_ids = jnp.where(edge_ids < 0, EDGE_DEV, edge_ids).astype(jnp.int32)
        summed = jax.ops.segment_sum(partial_value.reshape(-1, 2, NRHS), edge_ids.reshape(-1), num_segments=EDGE_DEV + 1)
        return summed[:EDGE_DEV]

    edge_sum = lax.map(owner_sums, jnp.arange(N_LEAF))
    lower_ids = shared_edges[:, 0]
    upper_ids = shared_edges[:, 1]
    lower_vals = edge_sum[source_rows, lower_ids]
    upper_vals = edge_sum[source_rows, upper_ids]
    zero_block = jnp.zeros_like(lower_vals[:1])
    from_below = jnp.concatenate([zero_block, upper_vals[:-1]], axis=0)
    from_above = jnp.concatenate([lower_vals[1:], zero_block], axis=0)
    total = edge_sum.at[source_rows, lower_ids].add(from_below).at[source_rows, upper_ids].add(from_above)
    return jnp.transpose(total, (2, 3, 0, 1)).reshape(2, NRHS, N_LEAF * EDGE_DEV)
```

```python
import functools

import jax
import jax.numpy as jnp
from jax import lax
from jax.experimental import pallas as pl
from jax.experimental.pallas import tpu as pltpu
from jax.sharding import PartitionSpec as P

QUAD = 12
TRI_LEAF = 32
EDGE_DEV = 384
LANES = 128
GROUP = 16
MESH = pl.DeviceIdType.MESH
F32 = jnp.float32
BF16 = jnp.bfloat16
NT = (((1,), (1,)), ((), ()))


def iota(shape, dim):
    return lax.broadcasted_iota(jnp.int32, shape, dim)


def bits(mask):
    return jnp.where(mask, 1.0, 0.0).astype(BF16)


def dot(a, b):
    return jnp.dot(a, b, preferred_element_type=F32)


def split(x):
    hi = x.astype(BF16)
    lo = (x - hi.astype(F32)).astype(BF16)
    return hi, lo


def column(row):
    k = row.shape[1]
    eye = iota((k, k), 0) == iota((k, k), 1)
    return jnp.sum(jnp.where(eye, jnp.broadcast_to(row, (k, k)), 0), axis=1, keepdims=True)


def kernel(
    peers, cap, capp, leaves, rhs, share,
    coef_hbm, op_hbm, map_ref, weight_hbm, edge_ref, shared_ref,
    out_ref,
    coef, op, field, wpad, wbuf, route, collect, sel_x, col_x, p_own, p_send, p_recv,
    send, recv, rim, rim_low, rim_up,
    coef_sem, op_sem, wpad_sem, wown_sem, wsend_sem, wrecv_sem, psend_sem, precv_sem,
    send_sem, recv_sem, rim_send, rim_recv,
):
    me = lax.axis_index("leaf")
    core = lax.axis_index("cone")
    points = 2 * QUAD * TRI_LEAF
    tris = leaves * TRI_LEAF
    half = rhs // 2
    width = GROUP * LANES
    groups = peers // GROUP

    coef_copy = pltpu.make_async_copy(coef_hbm, coef, coef_sem)
    coef_copy.start()
    op_copies = []
    for l in range(leaves):
        copy = pltpu.make_async_copy(op_hbm.at[l], op.at[l], op_sem.at[l])
        copy.start()
        op_copies.append(copy)

    rim_low[...] = jnp.zeros_like(rim_low)
    rim_up[...] = jnp.zeros_like(rim_up)
    barrier = pltpu.get_barrier_semaphore()

    def greet(k, carry):
        pl.semaphore_signal(
            barrier, inc=1, device_id=(lax.rem(me + k, peers), core), device_id_type=MESH
        )
        return carry

    lax.fori_loop(1, peers, greet, 0)
    pl.semaphore_signal(barrier, inc=1, device_id=(me, 1 - core), device_id_type=MESH)

    if capp == cap:
        weight_src = weight_hbm.at[0]
    else:
        wpad[...] = jnp.zeros_like(wpad)
        rows = pltpu.make_async_copy(weight_hbm.at[0], wpad.at[:, :cap], wpad_sem)
        rows.start()
        rows.wait()
        weight_src = wpad
    own_weights = pltpu.make_async_copy(weight_src.at[me], wbuf.at[me], wown_sem)
    own_weights.start()

    pl.semaphore_wait(barrier, peers)

    def weight_copy(k):
        to = lax.rem(me + k, peers)
        return pltpu.make_async_remote_copy(
            src_ref=weight_src.at[to], dst_ref=wbuf.at[me],
            send_sem=wsend_sem.at[to], recv_sem=wrecv_sem.at[me],
            device_id=(to, core), device_id_type=MESH,
        )

    def weight_arrival(k):
        source = lax.rem(me + k, peers)
        return pltpu.make_async_remote_copy(
            src_ref=weight_src.at[source], dst_ref=wbuf.at[source],
            send_sem=wsend_sem.at[source], recv_sem=wrecv_sem.at[source],
            device_id=(source, core), device_id_type=MESH,
        )

    def start_weight(k, carry):
        weight_copy(k).start()
        return carry

    lax.fori_loop(1, peers, start_weight, 0)

    maps = map_ref[0]
    filler = jnp.full((peers, LANES - 3 * cap), -1, jnp.int32)
    sel_x[...] = jnp.concatenate([maps, maps, maps, filler], axis=1)
    col_x[...] = jnp.concatenate([edge_ref[0, 0], edge_ref[1, 0], edge_ref[2, 0], filler], axis=1)
    lower_col = column(shared_ref[0, 0:1, :])
    upper_col = column(shared_ref[0, 1:2, :])
    rim_cols = jnp.concatenate(
        [lower_col, upper_col, jnp.full((LANES - 2 * share, 1), -2, jnp.int32)], axis=0
    )
    lane_e = iota((1, LANES), 1)

    def build_route(g):
        for j in range(GROUP):
            row = sel_x[pl.ds(g * GROUP + j, 1), :]
            for e in range(3):
                ours = jnp.logical_and(lane_e >= e * cap, lane_e < (e + 1) * cap)
                key = jnp.where(ours, row, -1)
                route[e * tris:(e + 1) * tris, j * LANES:(j + 1) * LANES] = bits(
                    iota((tris, LANES), 0) == key
                )

    def build_collect(g):
        for j in range(GROUP):
            row = col_x[pl.ds(g * GROUP + j, 1), :]
            lanes = slice(j * LANES, (j + 1) * LANES)
            collect[:EDGE_DEV, lanes] = bits(iota((EDGE_DEV, LANES), 0) == row)
            collect[EDGE_DEV:, lanes] = bits(rim_cols == row)

    if groups == 1:
        build_route(0)
        build_collect(0)

    coef_copy.wait()
    for l in range(leaves):
        op_copies[l].wait()
        total = None
        for k in range(coef.shape[1]):
            term = dot(coef[l, k].reshape(3 * rhs, -1), op[l, k])
            total = term if total is None else total + term
        field[l] = total

    own_weights.wait()

    def take_weight(k, carry):
        weight_arrival(k).wait_recv()
        return carry

    lax.fori_loop(1, peers, take_weight, 0)
    if capp != cap:
        maps = jnp.concatenate([maps, jnp.full((peers, capp - cap), -1, jnp.int32)], axis=1)
    slots = jnp.concatenate([maps[d:d + 1] for d in range(peers)], axis=1)
    pick = bits(iota((tris, peers * capp), 0) == slots)
    by_tri = dot(pick, wbuf[...].reshape(peers * capp, -1)).astype(BF16)
    rows = iota((16 * QUAD, 9 * QUAD), 0)
    point, pair = rows >> 4, rows & 15
    e_of = (pair * 11) >> 5
    order = (pair < 9) & (iota(rows.shape, 1) == e_of * (3 * QUAD) + point * 3 + pair - 3 * e_of)
    turned = lax.dot_general(bits(order), by_tri, NT, preferred_element_type=F32).astype(BF16)
    tri_row = (iota((tris, points), 0) & (TRI_LEAF - 1)) * (2 * QUAD)
    lane_q = iota((tris, points), 1)
    spread = bits((lane_q >= tri_row) & (lane_q < tri_row + 2 * QUAD))
    q_row = iota((1, points), 1)
    point_of = (q_row - ((q_row * 2731) >> 16) * (2 * QUAD)) >> 1
    q_col = iota((points, 2 * LANES), 0)
    out_lane = iota((points, 2 * LANES), 1)
    first = (out_lane & (TRI_LEAF - 1)) * (2 * QUAD)
    gather = bits(
        (q_col >= first) & (q_col < first + 2 * QUAD) & ((q_col & 1) == (out_lane >> 7))
    )
    tri_lane = iota((1, tris), 1)
    lane_group = iota((1, LANES), 1) // TRI_LEAF

    per_tile = LANES // TRI_LEAF
    tiles = tris // LANES
    acc = None
    for l in range(leaves):
        mine = jnp.where((tri_lane >= l * TRI_LEAF) & (tri_lane < (l + 1) * TRI_LEAF), turned, 0)
        wide = dot(mine, spread)
        weights = None
        for p in range(QUAD):
            part = jnp.where(point_of == p, wide[p * 16:(p + 1) * 16], 0.0)
            weights = part if weights is None else weights + part
        scaled = []
        for e in range(3):
            value = None
            for c in range(3):
                term = field[l, c * rhs:(c + 1) * rhs, :] * weights[3 * e + c:3 * e + c + 1, :]
                value = term if value is None else value + term
            scaled.append(value)
        hi, lo = split(jnp.concatenate(scaled, axis=0))
        summed = dot(hi, gather) + dot(lo, gather)
        keep = jnp.where(lane_group == l % per_tile, 1.0, 0.0)
        parts = [summed[:, :LANES] * keep, summed[:, LANES:] * keep]
        acc = parts if l % per_tile == 0 else [a + b for a, b in zip(acc, parts)]
        if l % per_tile == per_tile - 1:
            for e in range(3):
                at = e * tris + (l // per_tile) * LANES
                for i in range(2):
                    for c in range(2):
                        block = acc[i][e * rhs + c * half:e * rhs + (c + 1) * half]
                        p_own[c, i * half:(i + 1) * half, at:at + LANES] = block

    p_send[...] = p_own[1 - core]
    swap = pltpu.make_async_remote_copy(
        src_ref=p_send, dst_ref=p_recv, send_sem=psend_sem, recv_sem=precv_sem,
        device_id=(me, 1 - core), device_id_type=MESH,
    )
    swap.start()
    swap.wait_recv()
    ready = (p_own[core] + p_recv[...]).astype(BF16)

    def fill(g):
        routed = dot(ready, route[...]).astype(BF16)
        for j in range(GROUP):
            send[g * GROUP + j] = routed[:, j * LANES:(j + 1) * LANES]

    if groups == 1:
        fill(0)
    else:
        def fill_step(g, carry):
            build_route(g)
            fill(g)
            return carry

        lax.fori_loop(0, groups, fill_step, 0)

    def block_copy(k):
        to = lax.rem(me + k, peers)
        return pltpu.make_async_remote_copy(
            src_ref=send.at[to], dst_ref=recv.at[me],
            send_sem=send_sem.at[to], recv_sem=recv_sem.at[me],
            device_id=(to, core), device_id_type=MESH,
        )

    def block_arrival(k):
        source = lax.rem(me + k, peers)
        return pltpu.make_async_remote_copy(
            src_ref=send.at[source], dst_ref=recv.at[source],
            send_sem=send_sem.at[source], recv_sem=recv_sem.at[source],
            device_id=(source, core), device_id_type=MESH,
        )

    def start_block(k, carry):
        block_copy(k).start()
        return carry

    lax.fori_loop(1, peers, start_block, 0)
    recv[me] = send[me]

    scatter_ids = jnp.concatenate(
        [
            jnp.full((share, 1), -1, jnp.int32), lower_col,
            jnp.full((LANES - 2 * share, 1), -1, jnp.int32),
            upper_col, jnp.full((LANES - share, 1), -1, jnp.int32),
        ],
        axis=0,
    )
    scatter = bits(iota((2 * LANES, EDGE_DEV), 1) == scatter_ids)

    def take_block(k, carry):
        block_arrival(k).wait_recv()
        return carry

    lax.fori_loop(1, peers, take_block, 0)

    def gathered(g):
        lhs = jnp.concatenate([recv[g * GROUP + j] for j in range(GROUP)], axis=1)
        return lax.dot_general(lhs, collect[...], NT, preferred_element_type=F32)

    if groups == 1:
        edges = gathered(0)
    else:
        def gather_step(g, total):
            build_collect(g)
            return total + gathered(g)

        edges = lax.fori_loop(
            0, groups, gather_step, jnp.zeros((2 * half, EDGE_DEV + LANES), F32)
        )

    rim[...] = edges[:, EDGE_DEV:]
    up = pltpu.make_async_remote_copy(
        src_ref=rim, dst_ref=rim_low, send_sem=rim_send.at[0], recv_sem=rim_recv.at[0],
        device_id=(jnp.minimum(me + 1, peers - 1), core), device_id_type=MESH,
    )
    down = pltpu.make_async_remote_copy(
        src_ref=rim, dst_ref=rim_up, send_sem=rim_send.at[1], recv_sem=rim_recv.at[1],
        device_id=(jnp.maximum(me - 1, 0), core), device_id_type=MESH,
    )
    has_up, has_down = me < peers - 1, me > 0
    pl.when(has_up)(up.start)
    pl.when(has_down)(down.start)
    pl.when(has_down)(up.wait_recv)
    pl.when(has_up)(down.wait_recv)
    hi, lo = split(jnp.concatenate([rim_low[...], rim_up[...]], axis=1))
    total = edges[:, :EDGE_DEV] + dot(hi, scatter) + dot(lo, scatter)
    out_ref[0] = total[:half]
    out_ref[1] = total[half:]

    pl.when(has_up)(up.wait_send)
    pl.when(has_down)(down.wait_send)
    swap.wait_send()

    def sent(k, carry):
        weight_copy(k).wait_send()
        block_copy(k).wait_send()
        return carry

    lax.fori_loop(1, peers, sent, 0)


def body(coefficients, local_to_target, send_map, test_weight, slot_edge, shared_edges):
    peers, cap = send_map.shape[1], send_map.shape[2]
    leaves, cones, comps, rhs, r = coefficients.shape
    points = local_to_target.shape[3]
    share = shared_edges.shape[2]
    capp = max(cap, 16)
    tris = leaves * TRI_LEAF
    half = rhs // 2
    width = GROUP * LANES
    any_spec = pl.BlockSpec(memory_space=pl.ANY)
    vmem_spec = pl.BlockSpec(memory_space=pltpu.VMEM)
    dma = pltpu.SemaphoreType.DMA
    return pl.pallas_call(
        functools.partial(kernel, peers, cap, capp, leaves, rhs, share),
        out_shape=jax.ShapeDtypeStruct((2, half, EDGE_DEV), F32),
        in_specs=[any_spec, any_spec, vmem_spec, any_spec, vmem_spec, vmem_spec],
        out_specs=vmem_spec,
        scratch_shapes=[
            pltpu.VMEM(coefficients.shape, BF16),
            pltpu.VMEM(local_to_target.shape, BF16),
            pltpu.VMEM((leaves, comps * rhs, points), F32),
            pltpu.VMEM((peers, capp, 9 * QUAD) if capp != cap else (1, 16, LANES), BF16),
            pltpu.VMEM((peers, capp, 9 * QUAD), BF16),
            pltpu.VMEM((3 * tris, width), BF16),
            pltpu.VMEM((EDGE_DEV + LANES, width), BF16),
            pltpu.VMEM((peers, LANES), jnp.int32),
            pltpu.VMEM((peers, LANES), jnp.int32),
            pltpu.VMEM((2, 2 * half, 3 * tris), F32),
            pltpu.VMEM((2 * half, 3 * tris), F32),
            pltpu.VMEM((2 * half, 3 * tris), F32),
            pltpu.VMEM((peers, 2 * half, LANES), BF16),
            pltpu.VMEM((peers, 2 * half, LANES), BF16),
            pltpu.VMEM((2 * half, LANES), F32),
            pltpu.VMEM((2 * half, LANES), F32),
            pltpu.VMEM((2 * half, LANES), F32),
            dma, dma((leaves,)), dma, dma, dma((peers,)), dma((peers,)), dma, dma,
            dma((peers,)), dma((peers,)), dma((2,)), dma((2,)),
        ],
        compiler_params=pltpu.CompilerParams(
            collective_id=0, has_side_effects=True, vmem_limit_bytes=48 * 1024 * 1024
        ),
    )(coefficients, local_to_target, send_map, test_weight, slot_edge, shared_edges)


def solution(mesh):
    placed = (
        P("leaf", "cone", None, None, None),
        P("leaf", "cone", None, None),
        P("leaf", None, None),
        P("leaf", None, None, None),
        P(None, "leaf", None, None),
        P("leaf", None, None),
    )
    return jax.shard_map(
        body, mesh=mesh, in_specs=placed, out_specs=P(None, "cone", "leaf"), check_vma=False
    )
```

```python
import functools

import jax
import jax.numpy as jnp
from jax import lax
from jax.experimental import pallas as pl
from jax.experimental.pallas import tpu as pltpu
from jax.sharding import PartitionSpec as P

QUAD = 12
TRI_LEAF = 32
EDGE_DEV = 384
LANES = 128
GROUP = 16
MESH = pl.DeviceIdType.MESH
F32 = jnp.float32
BF16 = jnp.bfloat16
NT = (((1,), (1,)), ((), ()))


def iota(shape, dim):
    return lax.broadcasted_iota(jnp.int32, shape, dim)


def bits(mask):
    return jnp.where(mask, 1.0, 0.0).astype(BF16)


def dot(a, b):
    return jnp.dot(a, b, preferred_element_type=F32)


def split(x):
    hi = x.astype(BF16)
    lo = (x - hi.astype(F32)).astype(BF16)
    return hi, lo


def column(row):
    k = row.shape[1]
    eye = iota((k, k), 0) == iota((k, k), 1)
    return jnp.sum(jnp.where(eye, jnp.broadcast_to(row, (k, k)), 0), axis=1, keepdims=True)


def kernel(
    peers, cap, capp, leaves, rhs, share,
    coef_hbm, op_hbm, map_hbm, weight_hbm, edge_hbm, shared_hbm,
    out_ref,
    map_ref, edge_ref, shared_ref, coef, op, field, wpad, wbuf, route, collect, sel_x, col_x, p_own, p_send, p_recv,
    send, recv, rim, rim_low, rim_up,
    map_sem, edge_sem, shared_sem, coef_sem, op_sem, wpad_sem, wown_sem, wsend_sem, wrecv_sem, psend_sem, precv_sem,
    send_sem, recv_sem, rim_send, rim_recv,
):
    me = lax.axis_index("leaf")
    core = lax.axis_index("cone")
    points = 2 * QUAD * TRI_LEAF
    tris = leaves * TRI_LEAF
    half = rhs // 2
    groups = peers // GROUP

    coef_copy = pltpu.make_async_copy(coef_hbm, coef, coef_sem)
    coef_copy.start()
    small = [
        pltpu.make_async_copy(map_hbm, map_ref, map_sem),
        pltpu.make_async_copy(edge_hbm, edge_ref, edge_sem),
        pltpu.make_async_copy(shared_hbm, shared_ref, shared_sem),
    ]
    for copy in small:
        copy.start()
    op_copies = []
    for l in range(leaves):
        copy = pltpu.make_async_copy(op_hbm.at[l], op.at[l], op_sem.at[l])
        copy.start()
        op_copies.append(copy)

    rim_low[...] = jnp.zeros_like(rim_low)
    rim_up[...] = jnp.zeros_like(rim_up)
    barrier = pltpu.get_barrier_semaphore()

    def greet(k, carry):
        pl.semaphore_signal(
            barrier, inc=1, device_id=(lax.rem(me + k, peers), core), device_id_type=MESH
        )
        return carry

    lax.fori_loop(1, peers, greet, 0)
    pl.semaphore_signal(barrier, inc=1, device_id=(me, 1 - core), device_id_type=MESH)

    if capp == cap:
        weight_src = weight_hbm.at[0]
    else:
        wpad[...] = jnp.zeros_like(wpad)
        rows = pltpu.make_async_copy(weight_hbm.at[0], wpad.at[:, :cap], wpad_sem)
        rows.start()
        rows.wait()
        weight_src = wpad
    own_weights = pltpu.make_async_copy(weight_src.at[me], wbuf.at[me], wown_sem)
    own_weights.start()

    rows = iota((16 * QUAD, 9 * QUAD), 0)
    point, pair = rows >> 4, rows & 15
    e_of = (pair * 11) >> 5
    order = bits((pair < 9) & (iota(rows.shape, 1) == e_of * (3 * QUAD) + point * 3 + pair - 3 * e_of))
    tri_row = (iota((tris, points), 0) & (TRI_LEAF - 1)) * (2 * QUAD)
    lane_q = iota((tris, points), 1)
    spread = bits((lane_q >= tri_row) & (lane_q < tri_row + 2 * QUAD))
    q_row = iota((1, points), 1)
    point_of = (q_row - ((q_row * 2731) >> 16) * (2 * QUAD)) >> 1
    q_col = iota((points, 2 * LANES), 0)
    out_lane = iota((points, 2 * LANES), 1)
    first = (out_lane & (TRI_LEAF - 1)) * (2 * QUAD)
    gather = bits(
        (q_col >= first) & (q_col < first + 2 * QUAD) & ((q_col & 1) == (out_lane >> 7))
    )
    tri_lane = iota((1, tris), 1)
    lane_group = iota((1, LANES), 1) // TRI_LEAF

    small[0].wait()
    maps = map_ref[0]
    filler = jnp.full((peers, LANES - 3 * cap), -1, jnp.int32)
    sel_x[...] = jnp.concatenate([maps, maps, maps, filler], axis=1)
    if capp != cap:
        maps = jnp.concatenate([maps, jnp.full((peers, capp - cap), -1, jnp.int32)], axis=1)
    slots = jnp.concatenate([maps[d:d + 1] for d in range(peers)], axis=1)
    pick = bits(iota((tris, peers * capp), 0) == slots)
    small[1].wait()
    small[2].wait()
    col_x[...] = jnp.concatenate([edge_ref[0, 0], edge_ref[1, 0], edge_ref[2, 0], filler], axis=1)
    lower_col = column(shared_ref[0, 0:1, :])
    upper_col = column(shared_ref[0, 1:2, :])
    rim_cols = jnp.concatenate(
        [lower_col, upper_col, jnp.full((LANES - 2 * share, 1), -2, jnp.int32)], axis=0
    )
    lane_e = iota((1, LANES), 1)
    per_tile = LANES // TRI_LEAF
    tiles = tris // LANES

    def build_route(g):
        for j in range(GROUP):
            row = sel_x[pl.ds(g * GROUP + j, 1), :]
            for e in range(3):
                ours = jnp.logical_and(lane_e >= e * cap, lane_e < (e + 1) * cap)
                key = jnp.where(ours, row, -1)
                for t in range(tiles):
                    at = (t * 3 + e) * LANES
                    route[at:at + LANES, j * LANES:(j + 1) * LANES] = bits(
                        iota((LANES, LANES), 0) + t * LANES == key
                    )

    def build_collect(g):
        for j in range(GROUP):
            row = col_x[pl.ds(g * GROUP + j, 1), :]
            lanes = slice(j * LANES, (j + 1) * LANES)
            collect[:EDGE_DEV, lanes] = bits(iota((EDGE_DEV, LANES), 0) == row)
            collect[EDGE_DEV:, lanes] = bits(rim_cols == row)

    pl.semaphore_wait(barrier, peers)

    def weight_copy(k):
        to = lax.rem(me + k, peers)
        return pltpu.make_async_remote_copy(
            src_ref=weight_src.at[to], dst_ref=wbuf.at[me],
            send_sem=wsend_sem.at[to], recv_sem=wrecv_sem.at[me],
            device_id=(to, core), device_id_type=MESH,
        )

    def weight_arrival(k):
        source = lax.rem(me + k, peers)
        return pltpu.make_async_remote_copy(
            src_ref=weight_src.at[source], dst_ref=wbuf.at[source],
            send_sem=wsend_sem.at[source], recv_sem=wrecv_sem.at[source],
            device_id=(source, core), device_id_type=MESH,
        )

    def start_weight(k, carry):
        weight_copy(k).start()
        return carry

    lax.fori_loop(1, peers, start_weight, 0)

    coef_copy.wait()
    for l in range(leaves):
        op_copies[l].wait()
        total = None
        for k in range(coef.shape[1]):
            term = dot(coef[l, k].reshape(3 * rhs, -1), op[l, k])
            total = term if total is None else total + term
        field[l] = total

    own_weights.wait()

    def take_weight(k, carry):
        weight_arrival(k).wait_recv()
        return carry

    lax.fori_loop(1, peers, take_weight, 0)
    by_tri = dot(pick, wbuf[...].reshape(peers * capp, -1)).astype(BF16)
    turned = lax.dot_general(order, by_tri, NT, preferred_element_type=F32).astype(BF16)
    acc = None
    swaps = []
    for l in range(leaves):
        mine = jnp.where((tri_lane >= l * TRI_LEAF) & (tri_lane < (l + 1) * TRI_LEAF), turned, 0)
        wide = dot(mine, spread)
        weights = None
        for p in range(QUAD):
            part = jnp.where(point_of == p, wide[p * 16:(p + 1) * 16], 0.0)
            weights = part if weights is None else weights + part
        scaled = []
        for e in range(3):
            value = None
            for c in range(3):
                term = field[l, c * rhs:(c + 1) * rhs, :] * weights[3 * e + c:3 * e + c + 1, :]
                value = term if value is None else value + term
            scaled.append(value)
        hi, lo = split(jnp.concatenate(scaled, axis=0))
        summed = dot(hi, gather) + dot(lo, gather)
        keep = jnp.where(lane_group == l % per_tile, 1.0, 0.0)
        parts = [summed[:, :LANES] * keep, summed[:, LANES:] * keep]
        acc = parts if l % per_tile == 0 else [a + b for a, b in zip(acc, parts)]
        if l % per_tile == per_tile - 1:
            tile = l // per_tile
            for e in range(3):
                for i in range(2):
                    for c in range(2):
                        block = acc[i][e * rhs + c * half:e * rhs + (c + 1) * half]
                        p_own[c, tile, i * half:(i + 1) * half, e * LANES:(e + 1) * LANES] = block

            p_send[tile] = p_own[1 - core, tile]
            swap = pltpu.make_async_remote_copy(
                src_ref=p_send.at[tile], dst_ref=p_recv.at[tile],
                send_sem=psend_sem.at[tile], recv_sem=precv_sem.at[tile],
                device_id=(me, 1 - core), device_id_type=MESH,
            )
            swap.start()
            swaps.append(swap)

    if groups == 1:
        build_route(0)
    sums = []
    for tile in range(tiles):
        swaps[tile].wait_recv()
        sums.append((p_own[core, tile] + p_recv[tile]).astype(BF16))
    ready = jnp.concatenate(sums, axis=1)

    def fill(g):
        routed = dot(ready, route[...]).astype(BF16)
        for j in range(GROUP):
            send[g * GROUP + j] = routed[:, j * LANES:(j + 1) * LANES]

    if groups == 1:
        fill(0)
    else:
        def fill_step(g, carry):
            build_route(g)
            fill(g)
            return carry

        lax.fori_loop(0, groups, fill_step, 0)

    def block_copy(k):
        to = lax.rem(me + k, peers)
        return pltpu.make_async_remote_copy(
            src_ref=send.at[to], dst_ref=recv.at[me],
            send_sem=send_sem.at[to], recv_sem=recv_sem.at[me],
            device_id=(to, core), device_id_type=MESH,
        )

    def block_arrival(k):
        source = lax.rem(me + k, peers)
        return pltpu.make_async_remote_copy(
            src_ref=send.at[source], dst_ref=recv.at[source],
            send_sem=send_sem.at[source], recv_sem=recv_sem.at[source],
            device_id=(source, core), device_id_type=MESH,
        )

    def start_block(k, carry):
        block_copy(k).start()
        return carry

    lax.fori_loop(1, peers, start_block, 0)
    recv[me] = send[me]
    if groups == 1:
        build_collect(0)

    scatter_ids = jnp.concatenate(
        [
            jnp.full((share, 1), -1, jnp.int32), lower_col,
            jnp.full((LANES - 2 * share, 1), -1, jnp.int32),
            upper_col, jnp.full((LANES - share, 1), -1, jnp.int32),
        ],
        axis=0,
    )
    scatter = bits(iota((2 * LANES, EDGE_DEV), 1) == scatter_ids)

    def take_block(k, carry):
        block_arrival(k).wait_recv()
        return carry

    lax.fori_loop(1, peers, take_block, 0)

    def gathered(g):
        lhs = jnp.concatenate([recv[g * GROUP + j] for j in range(GROUP)], axis=1)
        return lax.dot_general(lhs, collect[...], NT, preferred_element_type=F32)

    if groups == 1:
        edges = gathered(0)
    else:
        def gather_step(g, total):
            build_collect(g)
            return total + gathered(g)

        edges = lax.fori_loop(
            0, groups, gather_step, jnp.zeros((2 * half, EDGE_DEV + LANES), F32)
        )

    rim[...] = edges[:, EDGE_DEV:]
    up = pltpu.make_async_remote_copy(
        src_ref=rim, dst_ref=rim_low, send_sem=rim_send.at[0], recv_sem=rim_recv.at[0],
        device_id=(jnp.minimum(me + 1, peers - 1), core), device_id_type=MESH,
    )
    down = pltpu.make_async_remote_copy(
        src_ref=rim, dst_ref=rim_up, send_sem=rim_send.at[1], recv_sem=rim_recv.at[1],
        device_id=(jnp.maximum(me - 1, 0), core), device_id_type=MESH,
    )
    has_up, has_down = me < peers - 1, me > 0
    pl.when(has_up)(up.start)
    pl.when(has_down)(down.start)
    pl.when(has_down)(up.wait_recv)
    pl.when(has_up)(down.wait_recv)
    hi, lo = split(jnp.concatenate([rim_low[...], rim_up[...]], axis=1))
    total = edges[:, :EDGE_DEV] + dot(hi, scatter) + dot(lo, scatter)
    out_ref[0] = total[:half]
    out_ref[1] = total[half:]

    pl.when(has_up)(up.wait_send)
    pl.when(has_down)(down.wait_send)
    for swap in swaps:
        swap.wait_send()

    def sent(k, carry):
        weight_copy(k).wait_send()
        block_copy(k).wait_send()
        return carry

    lax.fori_loop(1, peers, sent, 0)


def body(coefficients, local_to_target, send_map, test_weight, slot_edge, shared_edges):
    peers, cap = send_map.shape[1], send_map.shape[2]
    leaves, cones, comps, rhs, r = coefficients.shape
    points = local_to_target.shape[3]
    share = shared_edges.shape[2]
    capp = max(cap, 16)
    tris = leaves * TRI_LEAF
    half = rhs // 2
    width = GROUP * LANES
    any_spec = pl.BlockSpec(memory_space=pl.ANY)
    vmem_spec = pl.BlockSpec(memory_space=pltpu.VMEM)
    dma = pltpu.SemaphoreType.DMA
    return pl.pallas_call(
        functools.partial(kernel, peers, cap, capp, leaves, rhs, share),
        out_shape=jax.ShapeDtypeStruct((2, half, EDGE_DEV), F32),
        in_specs=[any_spec] * 6,
        out_specs=vmem_spec,
        scratch_shapes=[
            pltpu.VMEM(send_map.shape, jnp.int32),
            pltpu.VMEM(slot_edge.shape, jnp.int32),
            pltpu.VMEM(shared_edges.shape, jnp.int32),
            pltpu.VMEM(coefficients.shape, BF16),
            pltpu.VMEM(local_to_target.shape, BF16),
            pltpu.VMEM((leaves, comps * rhs, points), F32),
            pltpu.VMEM((peers, capp, 9 * QUAD) if capp != cap else (1, 16, LANES), BF16),
            pltpu.VMEM((peers, capp, 9 * QUAD), BF16),
            pltpu.VMEM((3 * tris, width), BF16),
            pltpu.VMEM((EDGE_DEV + LANES, width), BF16),
            pltpu.VMEM((peers, LANES), jnp.int32),
            pltpu.VMEM((peers, LANES), jnp.int32),
            pltpu.VMEM((2, tris // LANES, 2 * half, 3 * LANES), F32),
            pltpu.VMEM((tris // LANES, 2 * half, 3 * LANES), F32),
            pltpu.VMEM((tris // LANES, 2 * half, 3 * LANES), F32),
            pltpu.VMEM((peers, 2 * half, LANES), BF16),
            pltpu.VMEM((peers, 2 * half, LANES), BF16),
            pltpu.VMEM((2 * half, LANES), F32),
            pltpu.VMEM((2 * half, LANES), F32),
            pltpu.VMEM((2 * half, LANES), F32),
            dma, dma, dma, dma, dma((leaves,)), dma, dma, dma((peers,)), dma((peers,)),
            dma((tris // LANES,)), dma((tris // LANES,)),
            dma((peers,)), dma((peers,)), dma((2,)), dma((2,)),
        ],
        compiler_params=pltpu.CompilerParams(
            collective_id=0, has_side_effects=True, vmem_limit_bytes=60 * 1024 * 1024
        ),
    )(coefficients, local_to_target, send_map, test_weight, slot_edge, shared_edges)


def solution(mesh):
    placed = (
        P("leaf", "cone", None, None, None),
        P("leaf", "cone", None, None),
        P("leaf", None, None),
        P("leaf", None, None, None),
        P(None, "leaf", None, None),
        P("leaf", None, None),
    )
    return jax.shard_map(
        body, mesh=mesh, in_specs=placed, out_specs=P(None, "cone", "leaf"), check_vma=False
    )
```
